32 devices in a mesh: groups: 2 (over y), prow: 4 (over x, core), pcol: 4 (over z).
Axes of the slice: x: 2, y: 2, z: 4, core: 2. Of those that a mesh axis runs over, the one named last changes fastest.
Arguments:
- rhs: bfloat16 [8, 32, 2048], P('groups', None, 'pcol'), parts along dimension 0, may hold values from -6 to 6
- dinv: bfloat16 [8, 512, 2048], P('groups', None, 'pcol'), parts along dimension 0
- tiles: bfloat16 [128, 512, 512], P(('groups', 'prow', 'pcol')), parts along dimension 0, may hold values from -0.09375 to 0.09375
- tile_source: int32 [128], P(('groups', 'prow', 'pcol')), parts along dimension 0, may hold values from 0 to 11, as said below
- tile_target: int32 [128], P(('groups', 'prow', 'pcol')), parts along dimension 0, may hold values from -1 to 3, as said below
Outputs:
- solution: bfloat16 [8, 32, 2048], P('groups', None, 'pcol'), parts along dimension 0
The draws below stay inside these ranges and needn't reach their ends.
There are 2 independent parts, one for each index of `groups`. The reference program is written for one: setup_inputs(seed, part) draws one part's arguments, and reference() takes and returns one part's arrays. A program takes and returns all parts, laid end to end along the dimension named above; each array names one. Nothing has to cross between parts.
Inputs may be any that keep to these rules, and one draw needn't show every extreme that they name: tile_source // 4 is smaller than tile_target in every filled slot. `tile_target`: -1 marks an empty slot; a grid position's filled slots come first; some positions fill all 4, others only one.
All inputs are finite; a program needn't handle non-finite values.
Results may differ from the reference program's by a relative error of at most 0.0055.
Values may be sent and summed in bfloat16 or wider, within the bound.
A program may use at most 64 MiB of HBM per device.

```python
import jax
import jax.numpy as jnp
from jax import lax

BS = 512
SAMPLES = 32
LEVELS = 4
SLOTS = 4
BLOCKS_LEVEL = 4
GRID = 16


def slot_plan(key):
    base = jax.random.fold_in(key, 11)
    key_a, key_b, key_c, key_d = jax.random.split(base, 4)
    target = jax.random.randint(key_a, (GRID, SLOTS), 1, LEVELS)
    source_level = jax.random.randint(key_b, (GRID, SLOTS), 0, 10000) % target
    column = jax.random.randint(key_c, (GRID, SLOTS), 0, BLOCKS_LEVEL)
    target = target.at[0, 0].set(LEVELS - 1).at[0, 1].set(1)
    source_level = source_level.at[0, 0].set(LEVELS - 2).at[0, 1].set(0)
    column = column.at[0, 0].set(BLOCKS_LEVEL - 1).at[0, 1].set(0)
    position = jnp.arange(GRID, dtype=jnp.int32)[:, None]
    count = jax.random.randint(key_d, (GRID, 1), 1, SLOTS + 1)
    count = jnp.where(position % 3 == 0, SLOTS, jnp.where(position == 1, 1, count))
    filled = jnp.arange(SLOTS, dtype=jnp.int32)[None, :] < count
    source = (source_level * BLOCKS_LEVEL + column).astype(jnp.int32)
    marked = jnp.where(filled, target, -1).astype(jnp.int32)
    return (source.reshape(-1), marked.reshape(-1))


def draw_tile_source(key, part):
    return slot_plan(key)[0]


def draw_tile_target(key, part):
    return slot_plan(key)[1]


def draw_dinv(key, part):
    key_a, key_b = jax.random.split(jax.random.fold_in(key, 3))
    shape = (LEVELS, BS, BLOCKS_LEVEL * BS)
    row_ids = lax.broadcasted_iota(jnp.int32, shape, 1)
    col_ids = lax.broadcasted_iota(jnp.int32, shape, 2) % BS
    diag = jax.random.uniform(key_a, shape, jnp.float32, 0.6, 1.4)
    off = jax.random.normal(key_b, shape, jnp.float32) * 0.5 * BS ** (-0.5)
    return jnp.where(row_ids == col_ids, diag, off).astype(jnp.bfloat16)


def steps_of(stream_key, dims, shards, low, high):
    factor_of = 1.0
    for axis_at, shards_of in shards:
        steps = jax.random.uniform(jax.random.fold_in(jax.random.fold_in(stream_key, 6), axis_at), (shards_of,), jnp.float32, low / len(shards), high / len(shards))
        factor_of = factor_of * jnp.repeat(jnp.exp(steps), dims[axis_at] // shards_of).reshape((-1,) + (1,) * (len(dims) - 1 - axis_at))
    return factor_of


def gaussian(stream_key, extent, width, most, shards=(), held_as=jnp.bfloat16):
    drawn = width * jax.random.normal(stream_key, extent, jnp.float32)
    if shards:
        drawn = drawn * steps_of(stream_key, extent, shards, -0.22, 0.18)
    return jnp.clip(drawn, -most, most).astype(held_as)


def setup_inputs(seed: int = 0, part: int = 0) -> dict:
    keys = jax.random.split(jax.random.key(seed), 6)
    own_keys = jax.random.split(jax.random.fold_in(keys[5], part), 6)
    return {
        "rhs": gaussian(own_keys[0], (LEVELS, SAMPLES, BLOCKS_LEVEL * BS), 1.0, 6.0, ((2, 4),)),
        "dinv": draw_dinv(jax.random.fold_in(jax.random.fold_in(keys[5], part), 71), part),
        "tiles": gaussian(own_keys[2], (GRID * SLOTS, BS, BS), (0.35 * BS ** -0.5), 0.09375, ((0, 16),)),
        "tile_source": draw_tile_source(jax.random.fold_in(jax.random.fold_in(keys[5], part), 71), part),
        "tile_target": draw_tile_target(jax.random.fold_in(jax.random.fold_in(keys[5], part), 71), part),
    }


def reference(rhs, dinv, tiles, tile_source, tile_target):
    columns = BLOCKS_LEVEL
    owner_col = ((jnp.arange(tiles.shape[0], dtype=jnp.int32) // SLOTS) % columns).astype(jnp.int32)
    partial_value = jnp.zeros((LEVELS, SAMPLES, columns * BS), jnp.float32)
    solved = []
    for level in range(LEVELS):
        short = rhs[level].astype(jnp.float32) - partial_value[level]
        rounded = lax.optimization_barrier(short.astype(jnp.bfloat16)).astype(jnp.float32)
        ys = rounded.reshape(SAMPLES, columns, BS)
        inverse = dinv[level].astype(jnp.float32).reshape(BS, columns, BS)
        block = jnp.einsum("scb,acb->sca", ys, inverse).reshape(SAMPLES, columns * BS).astype(jnp.bfloat16)
        solved.append(block)
        if level + 1 < LEVELS:
            def step(carry, item, level=level, block=block):
                tile, source, target, col_i = item
                active = (source // columns == level) & (target > level)

                def add(state):
                    start = ((source % columns) * BS).astype(jnp.int32)
                    src_block = lax.dynamic_slice_in_dim(block, start, BS, 1)
                    term = jnp.dot(src_block, tile.T, preferred_element_type=jnp.float32)
                    tgt = jnp.clip(target, 0, LEVELS - 1).astype(jnp.int32)
                    where = (tgt, jnp.int32(0), (col_i * BS).astype(jnp.int32))
                    current = lax.dynamic_slice(state, where, (1, SAMPLES, BS))
                    return lax.dynamic_update_slice(state, current + term[None], where)

                return lax.cond(active, add, lambda state: state, carry), None

            partial_value, _ = lax.scan(step, partial_value, (tiles, tile_source, tile_target, owner_col))
    return jnp.stack(solved)
```

```python
import jax
import jax.numpy as jnp
from jax import lax
from jax.experimental import pallas as pl
from jax.experimental.pallas import tpu as pltpu
from jax.sharding import PartitionSpec as P

MESH = pl.DeviceIdType.MESH


def apply_right(left, matrix):
    return lax.dot_general(
        left, matrix, (((1,), (1,)), ((), ())), preferred_element_type=jnp.float32
    )


def kernel(
    cols, rows, source_ref, target_ref, rhs_hbm, dinv_hbm, tiles_hbm, out_ref,
    rhs, dinv, tiles, picked, own, part, xs, local_sem, send_x, recv_x, send_p, recv_p,
):
    levels, slots = rhs.shape[0], tiles.shape[0]
    p, c = lax.axis_index("prow"), lax.axis_index("pcol")

    loads = [pltpu.make_async_copy(rhs_hbm, rhs, local_sem.at[0])]
    for level in range(levels):
        loads.append(
            pltpu.make_async_copy(dinv_hbm.at[level], dinv.at[level], local_sem.at[1 + level])
        )
    tile_load = pltpu.make_async_copy(tiles_hbm, tiles, local_sem.at[1 + levels])
    loads[0].start()
    loads[1].start()
    tile_load.start()
    for load in loads[2:]:
        load.start()

    barrier = pltpu.get_barrier_semaphore()
    for k in range(1, cols):
        pl.semaphore_signal(
            barrier, inc=1, device_id={"pcol": lax.rem(c + k, cols)}, device_id_type=MESH
        )
    for k in range(1, rows):
        pl.semaphore_signal(
            barrier, inc=1, device_id={"prow": lax.rem(p + k, rows)}, device_id_type=MESH
        )

    def send_block(level):
        copies = []
        for k in range(1, cols):
            copy = pltpu.make_async_remote_copy(
                src_ref=own.at[level],
                dst_ref=xs[level].at[c],
                send_sem=send_x.at[level, k],
                recv_sem=recv_x.at[level, k],
                device_id={"pcol": lax.rem(c + k, cols)},
                device_id_type=MESH,
            )
            copy.start()
            copies.append(copy)
        return copies

    def send_part(level):
        copies = []
        for k in range(1, rows):
            copy = pltpu.make_async_remote_copy(
                src_ref=part.at[level, p],
                dst_ref=part.at[level, p],
                send_sem=send_p.at[level, k],
                recv_sem=recv_p.at[level, k],
                device_id={"prow": lax.rem(p + k, rows)},
                device_id_type=MESH,
            )
            copy.start()
            copies.append(copy)
        return copies

    picked[...] = jnp.zeros_like(picked)
    src_level = [source_ref[g] // cols for g in range(slots)]
    src_col = [lax.rem(source_ref[g], cols) for g in range(slots)]
    pending = []
    for level in range(levels):
        if level == 0:
            loads[0].wait()
            short = rhs[0]
        else:
            partial_value = None
            for g in range(slots):
                now = jnp.where(
                    src_level[g] == level - 1, xs[level - 1][src_col[g]], picked[g]
                )
                picked[g] = now
                left = jnp.where(target_ref[g] == level, now, jnp.zeros_like(now))
                term = apply_right(left, tiles[g])
                partial_value = term if partial_value is None else partial_value + term
            part[level - 1, p] = partial_value
            copies = send_part(level - 1)
            for copy in copies:
                copy.wait_recv()
            pending += copies
            total = part[level - 1, 0]
            for q in range(1, rows):
                total = total + part[level - 1, q]
            short = (rhs[level].astype(jnp.float32) - total).astype(jnp.bfloat16)
        loads[1 + level].wait()
        block = apply_right(short, dinv[level]).astype(jnp.bfloat16)
        out_ref[level] = block
        if level + 1 < levels:
            own[level] = block
            xs[level][c] = block
            if level == 0:
                pl.semaphore_wait(barrier, cols + rows - 2)
            copies = send_block(level)
            if level == 0:
                tile_load.wait()
            for copy in copies:
                copy.wait_recv()
            pending += copies
    for copy in pending:
        copy.wait_send()


def solution(mesh):
    rows, cols = mesh.shape["prow"], mesh.shape["pcol"]

    def body(rhs, dinv, tiles, tile_source, tile_target):
        levels, samples, width = rhs.shape
        slots = tiles.shape[0]

        def call(source_ref, target_ref, rhs_hbm, dinv_hbm, tiles_hbm, out_ref,
                 rhs_v, dinv_v, tiles_v, picked, own, part, *rest):
            xs, sems = rest[: levels - 1], rest[levels - 1 :]
            kernel(cols, rows, source_ref, target_ref, rhs_hbm, dinv_hbm, tiles_hbm, out_ref,
                   rhs_v, dinv_v, tiles_v, picked, own, part, xs, *sems)

        return pl.pallas_call(
            call,
            out_shape=jax.ShapeDtypeStruct(rhs.shape, jnp.bfloat16),
            in_specs=[pl.BlockSpec(memory_space=pltpu.SMEM)] * 2
            + [pl.BlockSpec(memory_space=pl.ANY)] * 3,
            out_specs=pl.BlockSpec(memory_space=pltpu.VMEM),
            scratch_shapes=[
                pltpu.VMEM(rhs.shape, jnp.bfloat16),
                pltpu.VMEM(dinv.shape, jnp.bfloat16),
                pltpu.VMEM(tiles.shape, jnp.bfloat16),
                pltpu.VMEM((slots, samples, width), jnp.bfloat16),
                pltpu.VMEM((levels - 1, samples, width), jnp.bfloat16),
                pltpu.VMEM((levels - 1, rows, samples, width), jnp.float32),
            ]
            + [pltpu.VMEM((cols, samples, width), jnp.bfloat16)] * (levels - 1)
            + [
                pltpu.SemaphoreType.DMA((levels + 2,)),
                pltpu.SemaphoreType.DMA((levels - 1, cols)),
                pltpu.SemaphoreType.DMA((levels - 1, cols)),
                pltpu.SemaphoreType.DMA((levels - 1, rows)),
                pltpu.SemaphoreType.DMA((levels - 1, rows)),
            ],
            compiler_params=pltpu.CompilerParams(
                collective_id=0, has_side_effects=True, vmem_limit_bytes=40 * 1024 * 1024
            ),
        )(tile_source, tile_target, rhs, dinv, tiles)

    placed = (
        P("groups", None, "pcol"),
        P("groups", None, "pcol"),
        P(("groups", "prow", "pcol"), None, None),
        P(("groups", "prow", "pcol")),
        P(("groups", "prow", "pcol")),
    )
    return jax.shard_map(
        body, mesh=mesh, in_specs=placed, out_specs=P("groups", None, "pcol"), check_vma=False
    )
```

```python
import jax
import jax.numpy as jnp
from jax import lax
from jax.experimental import pallas as pl
from jax.experimental.pallas import tpu as pltpu
from jax.sharding import PartitionSpec as P

MESH = pl.DeviceIdType.MESH
PAIR = 2


def apply_right(left, matrix):
    return lax.dot_general(
        left, matrix, (((1,), (1,)), ((), ())), preferred_element_type=jnp.float32
    )


def kernel(
    cols, rows, source_hbm, target_hbm, rhs_hbm, dinv_hbm, tiles_hbm, out_ref,
    source, target, rhs, dinv, tiles, picked, first, halves, x0, ys, final,
    load_sem, tile_sem, send_tile, recv_tile, send_x0, recv_x0, send_y, recv_y,
    send_half, recv_half, send_final, recv_final,
):
    levels, samples = rhs.shape[0], rhs.shape[1]
    slots = tiles.shape[1]
    half = samples // PAIR
    sums = rows // PAIR
    p, c = lax.axis_index("prow"), lax.axis_index("pcol")
    k, xg = lax.rem(p, PAIR), p // PAIR
    mate = p + 1 - 2 * k
    mine = pl.ds(pl.multiple_of(k * half, half), half)

    def remote(src, dst, send, recv, prow, pcol):
        return pltpu.make_async_remote_copy(
            src_ref=src, dst_ref=dst, send_sem=send, recv_sem=recv,
            device_id={"prow": prow, "pcol": pcol}, device_id_type=MESH,
        )

    peers = []
    for dx in range(sums):
        for dc in range(cols):
            if dx or dc:
                peers.append((lax.rem(xg + dx, sums) * PAIR + k, lax.rem(c + dc, cols), dx, dc))
    column = [lax.rem(p + d, rows) for d in range(1, rows)]

    load_rhs = pltpu.make_async_copy(rhs_hbm, rhs, load_sem.at[0])
    load_dinv = [
        pltpu.make_async_copy(dinv_hbm.at[level], dinv.at[level], load_sem.at[1 + level])
        for level in range(levels)
    ]
    load_source = pltpu.make_async_copy(source_hbm, source.at[0], load_sem.at[1 + levels])
    load_target = pltpu.make_async_copy(target_hbm, target.at[0], load_sem.at[2 + levels])
    load_tile = [
        pltpu.make_async_copy(tiles_hbm.at[g], tiles.at[0, g], tile_sem.at[g])
        for g in range(slots)
    ]
    load_rhs.start()
    load_dinv[0].start()

    barrier = pltpu.get_barrier_semaphore()
    greeted = [(prow, pcol) for prow, pcol, dx, dc in peers]
    for d in range(1, rows):
        if d % PAIR:
            greeted.append((column[d - 1], c))
    for prow, pcol in greeted:
        pl.semaphore_signal(
            barrier, inc=1, device_id={"prow": prow, "pcol": pcol}, device_id_type=MESH
        )
    load_source.start()
    load_target.start()
    for load in load_tile + load_dinv[1:]:
        load.start()

    picked[...] = jnp.zeros_like(picked)
    load_rhs.wait()
    load_dinv[0].wait()
    block = apply_right(rhs[0], dinv[0]).astype(jnp.bfloat16)
    out_ref[0] = block
    first[...] = block
    x0[c] = first[mine]
    pl.semaphore_wait(barrier, len(greeted))

    pending = []
    arrivals = []
    for prow, pcol, dx, dc in peers:
        if dx == 0:
            copy = remote(x0.at[c], x0.at[c], send_x0.at[dc], recv_x0.at[dc], p, pcol)
            copy.start()
            arrivals.append(copy)
    pending += arrivals
    swap = [
        remote(source_hbm, source.at[1], send_tile.at[slots], recv_tile.at[slots], mate, c),
        remote(target_hbm, target.at[1], send_tile.at[slots + 1], recv_tile.at[slots + 1], mate, c),
    ] + [
        remote(tiles_hbm.at[g], tiles.at[1, g], send_tile.at[g], recv_tile.at[g], mate, c)
        for g in range(slots)
    ]
    for copy in swap:
        copy.start()
    pending += swap

    load_source.wait()
    load_target.wait()
    swap[0].wait_recv()
    swap[1].wait_recv()
    slot = [(j, g) for j in range(PAIR) for g in range(slots)]
    src_level = {s: source[s[0], s[1]] // cols for s in slot}
    src_col = {s: lax.rem(source[s[0], s[1]], cols) for s in slot}
    to_level = {s: target[s[0], s[1]] for s in slot}

    half_copies = []
    for level in range(1, levels):
        for copy in arrivals:
            copy.wait_recv()
        partial_value = None
        for s in slot:
            if level == 1:
                load_tile[s[1]].wait() if s[0] == 0 else swap[2 + s[1]].wait_recv()
                seen = x0[src_col[s]]
            else:
                seen = ys[level - 2][0, src_col[s]].astype(jnp.float32)
                for q in range(1, sums):
                    seen = seen + ys[level - 2][q, src_col[s]].astype(jnp.float32)
                seen = seen.astype(jnp.bfloat16)
            now = jnp.where(src_level[s] == level - 1, seen, picked[s])
            picked[s] = now
            left = jnp.where(to_level[s] == level, now, jnp.zeros_like(now))
            term = apply_right(left, tiles[s])
            partial_value = term if partial_value is None else partial_value + term
        if level + 1 < levels:
            begin = jnp.where(xg == 0, rhs[level, mine].astype(jnp.float32), 0.0)
            short = begin - partial_value
            high = short.astype(jnp.bfloat16)
            low = (short - high.astype(jnp.float32)).astype(jnp.bfloat16)
            load_dinv[level].wait()
            both = apply_right(jnp.concatenate([high, low], axis=0), dinv[level])
            y = ys[level - 1]
            y[xg, c] = (both[:half] + both[half:]).astype(jnp.bfloat16)
            arrivals = []
            for prow, pcol, dx, dc in peers:
                copy = remote(
                    y.at[xg, c], y.at[xg, c],
                    send_y.at[level - 1, dx, dc], recv_y.at[level - 1, dx, dc], prow, pcol,
                )
                copy.start()
                arrivals.append(copy)
            pending += arrivals
        else:
            final[p] = partial_value
            arrivals = []
            for d in range(1, rows):
                copy = remote(
                    final.at[p], final.at[p], send_final.at[d], recv_final.at[d], column[d - 1], c
                )
                copy.start()
                arrivals.append(copy)
            pending += arrivals
        if level >= 2:
            y = ys[level - 2]
            total = y[0, c].astype(jnp.float32)
            for q in range(1, sums):
                total = total + y[q, c].astype(jnp.float32)
            halves[level - 2, k] = total.astype(jnp.bfloat16)
            copy = remote(
                halves.at[level - 2, k], halves.at[level - 2, k],
                send_half.at[level - 2], recv_half.at[level - 2], mate, c,
            )
            copy.start()
            half_copies.append(copy)
    for level, copy in enumerate(half_copies):
        copy.wait_recv()
        for j in range(PAIR):
            out_ref[1 + level, j * half : (j + 1) * half] = halves[level, j]
    pending += half_copies
    load_dinv[levels - 1].wait()
    for copy in arrivals:
        copy.wait_recv()
    shorts = []
    for j in range(PAIR):
        total = final[j]
        for q in range(1, sums):
            total = total + final[q * PAIR + j]
        begin = rhs[levels - 1, j * half : (j + 1) * half].astype(jnp.float32)
        shorts.append((begin - total).astype(jnp.bfloat16))
    short = jnp.concatenate(shorts, axis=0)
    out_ref[levels - 1] = apply_right(short, dinv[levels - 1]).astype(jnp.bfloat16)
    for copy in pending:
        copy.wait_send()


def solution(mesh):
    rows, cols = mesh.shape["prow"], mesh.shape["pcol"]

    def body(rhs, dinv, tiles, tile_source, tile_target):
        levels, samples, width = rhs.shape
        slots = tiles.shape[0]
        half, sums = samples // PAIR, rows // PAIR

        def call(*refs):
            ins, scratch, rest = refs[:6], refs[6:15], refs[15:]
            ys, rest = rest[: levels - 2], rest[levels - 2 :]
            kernel(cols, rows, *ins, *scratch, ys, *rest)

        dma = pltpu.SemaphoreType.DMA
        return pl.pallas_call(
            call,
            out_shape=jax.ShapeDtypeStruct(rhs.shape, jnp.bfloat16),
            in_specs=[pl.BlockSpec(memory_space=pl.ANY)] * 5,
            out_specs=pl.BlockSpec(memory_space=pltpu.VMEM),
            scratch_shapes=[
                pltpu.SMEM((PAIR, slots), jnp.int32),
                pltpu.SMEM((PAIR, slots), jnp.int32),
                pltpu.VMEM(rhs.shape, jnp.bfloat16),
                pltpu.VMEM(dinv.shape, jnp.bfloat16),
                pltpu.VMEM((PAIR,) + tiles.shape, jnp.bfloat16),
                pltpu.VMEM((PAIR, slots, half, width), jnp.bfloat16),
                pltpu.VMEM((samples, width), jnp.bfloat16),
                pltpu.VMEM((levels - 2, PAIR, half, width), jnp.bfloat16),
                pltpu.VMEM((cols, half, width), jnp.bfloat16),
            ]
            + [pltpu.VMEM((sums, cols, half, width), jnp.bfloat16)] * (levels - 2)
            + [
                pltpu.VMEM((rows, half, width), jnp.float32),
                dma((levels + 3,)),
                dma((slots,)),
                dma((slots + 2,)),
                dma((slots + 2,)),
                dma((cols,)),
                dma((cols,)),
                dma((levels - 2, sums, cols)),
                dma((levels - 2, sums, cols)),
                dma((levels - 2,)),
                dma((levels - 2,)),
                dma((rows,)),
                dma((rows,)),
            ],
            compiler_params=pltpu.CompilerParams(
                collective_id=0, has_side_effects=True, vmem_limit_bytes=60 * 1024 * 1024
            ),
        )(tile_source, tile_target, rhs, dinv, tiles)

    placed = (
        P("groups", None, "pcol"),
        P("groups", None, "pcol"),
        P(("groups", "prow", "pcol"), None, None),
        P(("groups", "prow", "pcol")),
        P(("groups", "prow", "pcol")),
    )
    return jax.shard_map(
        body, mesh=mesh, in_specs=placed, out_specs=P("groups", None, "pcol"), check_vma=False
    )
```

```python
import jax
import jax.numpy as jnp
from jax import lax
from jax.experimental import pallas as pl
from jax.experimental.pallas import tpu as pltpu
from jax.sharding import PartitionSpec as P

MESH = pl.DeviceIdType.MESH
PAIR = 2


def apply_right(left, matrix):
    return lax.dot_general(
        left, matrix, (((1,), (1,)), ((), ())), preferred_element_type=jnp.float32
    )


def apply_plain(left, matrix):
    return jnp.dot(left, matrix, preferred_element_type=jnp.float32)


def kernel(
    cols, rows, source_hbm, target_hbm, rhs_hbm, dinv_hbm, tiles_hbm, out_ref,
    source, target, rhs, dinv, raw, tiles, picked, first, halves, x0, ys, final,
    load_sem, tile_sem, send_tile, recv_tile, send_x0, recv_x0, send_y, recv_y,
    send_half, recv_half, send_final, recv_final, vouch,
):
    levels, samples = rhs.shape[0], rhs.shape[1]
    slots = raw.shape[0]
    half = samples // PAIR
    sums = rows // PAIR
    p, c = lax.axis_index("prow"), lax.axis_index("pcol")
    k, xg = lax.rem(p, PAIR), p // PAIR
    mate = p + 1 - 2 * k
    mine = pl.ds(pl.multiple_of(k * half, half), half)

    def remote(src, dst, send, recv, prow, pcol):
        return pltpu.make_async_remote_copy(
            src_ref=src, dst_ref=dst, send_sem=send, recv_sem=recv,
            device_id={"prow": prow, "pcol": pcol}, device_id_type=MESH,
        )

    peers = []
    for dx in range(sums):
        for dc in range(cols):
            if dx or dc:
                peers.append((lax.rem(xg + dx, sums) * PAIR + k, lax.rem(c + dc, cols), dx, dc))
    peers = peers[::-1]
    column = [lax.rem(p + d, rows) for d in range(1, rows)]

    load_rhs = pltpu.make_async_copy(rhs_hbm, rhs, load_sem.at[0])
    load_dinv = [
        pltpu.make_async_copy(dinv_hbm.at[level], dinv.at[level], load_sem.at[1 + level])
        for level in range(levels)
    ]
    load_source = pltpu.make_async_copy(source_hbm, source.at[0], load_sem.at[1 + levels])
    load_target = pltpu.make_async_copy(target_hbm, target.at[0], load_sem.at[2 + levels])
    load_tile = [
        pltpu.make_async_copy(tiles_hbm.at[g], raw.at[g], tile_sem.at[g])
        for g in range(slots)
    ]
    load_rhs.start()
    load_dinv[0].start()

    barrier = pltpu.get_barrier_semaphore()
    greeted = [(prow, pcol) for prow, pcol, dx, dc in peers if dx == 0]
    greeted += [(prow, c) for prow in column]
    for prow, pcol in greeted:
        pl.semaphore_signal(
            barrier, inc=1, device_id={"prow": prow, "pcol": pcol}, device_id_type=MESH
        )
    load_source.start()
    load_target.start()
    for load in load_tile + load_dinv[1:]:
        load.start()

    picked[...] = jnp.zeros_like(picked)
    load_rhs.wait()
    load_dinv[0].wait()
    block = apply_right(rhs[0], dinv[0]).astype(jnp.bfloat16)
    out_ref[0] = block
    first[...] = block
    x0[c] = first[mine]
    for g in range(slots):
        load_tile[g].wait()
        tiles[0, g] = raw[g].T
    pl.semaphore_wait(barrier, len(greeted))

    pending = []
    arrivals = []
    for prow, pcol, dx, dc in peers:
        if dx == 0:
            copy = remote(x0.at[c], x0.at[c], send_x0.at[dc], recv_x0.at[dc], p, pcol)
            copy.start()
            arrivals.append(copy)
    pending += arrivals
    swap = [
        remote(source_hbm, source.at[1], send_tile.at[slots], recv_tile.at[slots], mate, c),
        remote(target_hbm, target.at[1], send_tile.at[slots + 1], recv_tile.at[slots + 1], mate, c),
    ] + [
        remote(tiles.at[0, g], tiles.at[1, g], send_tile.at[g], recv_tile.at[g], mate, c)
        for g in range(slots)
    ]
    for copy in swap:
        copy.start()
    for prow, pcol, dx, dc in peers:
        if dx and dc == 0:
            pl.semaphore_signal(
                vouch, inc=1, device_id={"prow": prow, "pcol": pcol}, device_id_type=MESH
            )
    pending += swap

    for level in range(1, levels):
        load_dinv[level].wait()
        dinv[level] = dinv[level].T
    load_source.wait()
    load_target.wait()
    swap[0].wait_recv()
    swap[1].wait_recv()
    slot = [(j, g) for j in range(PAIR) for g in range(slots)]
    src_level = {s: source[s[0], s[1]] // cols for s in slot}
    src_col = {s: lax.rem(source[s[0], s[1]], cols) for s in slot}
    to_level = {s: target[s[0], s[1]] for s in slot}

    half_copies = []
    for level in range(1, levels):
        for copy in arrivals:
            copy.wait_recv()
        partial_value = None
        for s in slot:
            if level == 1:
                if s[0] == 1:
                    swap[2 + s[1]].wait_recv()
                seen = x0[src_col[s]]
            else:
                seen = ys[level - 2][0, src_col[s]].astype(jnp.float32)
                for q in range(1, sums):
                    seen = seen + ys[level - 2][q, src_col[s]].astype(jnp.float32)
                seen = seen.astype(jnp.bfloat16)
            now = jnp.where(src_level[s] == level - 1, seen, picked[s])
            picked[s] = now
            left = jnp.where(to_level[s] == level, now, jnp.zeros_like(now))
            term = apply_plain(left, tiles[s])
            partial_value = term if partial_value is None else partial_value + term
        if level + 1 < levels:
            begin = jnp.where(xg == 0, rhs[level, mine].astype(jnp.float32), 0.0)
            short = begin - partial_value
            high = short.astype(jnp.bfloat16)
            low = (short - high.astype(jnp.float32)).astype(jnp.bfloat16)
            both = apply_plain(jnp.concatenate([high, low], axis=0), dinv[level])
            if level == 1:
                pl.semaphore_wait(vouch, sums - 1)
            y = ys[level - 1]
            y[xg, c] = (both[:half] + both[half:]).astype(jnp.bfloat16)
            arrivals = []
            for prow, pcol, dx, dc in peers:
                copy = remote(
                    y.at[xg, c], y.at[xg, c],
                    send_y.at[level - 1, dx, dc], recv_y.at[level - 1, dx, dc], prow, pcol,
                )
                copy.start()
                arrivals.append(copy)
            pending += arrivals
        else:
            final[p] = partial_value
            arrivals = []
            for d in range(1, rows):
                copy = remote(
                    final.at[p], final.at[p], send_final.at[d], recv_final.at[d], column[d - 1], c
                )
                copy.start()
                arrivals.append(copy)
            pending += arrivals
        if level >= 2:
            y = ys[level - 2]
            total = y[0, c].astype(jnp.float32)
            for q in range(1, sums):
                total = total + y[q, c].astype(jnp.float32)
            halves[level - 2, k] = total.astype(jnp.bfloat16)
            copy = remote(
                halves.at[level - 2, k], halves.at[level - 2, k],
                send_half.at[level - 2], recv_half.at[level - 2], mate, c,
            )
            copy.start()
            half_copies.append(copy)
    for level, copy in enumerate(half_copies):
        copy.wait_recv()
        for j in range(PAIR):
            out_ref[1 + level, j * half : (j + 1) * half] = halves[level, j]
    pending += half_copies
    for copy in arrivals:
        copy.wait_recv()
    shorts = []
    for j in range(PAIR):
        total = final[j]
        for q in range(1, sums):
            total = total + final[q * PAIR + j]
        begin = rhs[levels - 1, j * half : (j + 1) * half].astype(jnp.float32)
        shorts.append((begin - total).astype(jnp.bfloat16))
    short = jnp.concatenate(shorts, axis=0)
    out_ref[levels - 1] = apply_plain(short, dinv[levels - 1]).astype(jnp.bfloat16)
    for copy in pending:
        copy.wait_send()


def solution(mesh):
    rows, cols = mesh.shape["prow"], mesh.shape["pcol"]

    def body(rhs, dinv, tiles, tile_source, tile_target):
        levels, samples, width = rhs.shape
        slots = tiles.shape[0]
        half, sums = samples // PAIR, rows // PAIR

        def call(*refs):
            ins, scratch, rest = refs[:6], refs[6:16], refs[16:]
            ys, rest = rest[: levels - 2], rest[levels - 2 :]
            kernel(cols, rows, *ins, *scratch, ys, *rest)

        dma = pltpu.SemaphoreType.DMA
        return pl.pallas_call(
            call,
            out_shape=jax.ShapeDtypeStruct(rhs.shape, jnp.bfloat16),
            in_specs=[pl.BlockSpec(memory_space=pl.ANY)] * 5,
            out_specs=pl.BlockSpec(memory_space=pltpu.VMEM),
            scratch_shapes=[
                pltpu.SMEM((PAIR, slots), jnp.int32),
                pltpu.SMEM((PAIR, slots), jnp.int32),
                pltpu.VMEM(rhs.shape, jnp.bfloat16),
                pltpu.VMEM(dinv.shape, jnp.bfloat16),
                pltpu.VMEM(tiles.shape, jnp.bfloat16),
                pltpu.VMEM((PAIR,) + tiles.shape, jnp.bfloat16),
                pltpu.VMEM((PAIR, slots, half, width), jnp.bfloat16),
                pltpu.VMEM((samples, width), jnp.bfloat16),
                pltpu.VMEM((levels - 2, PAIR, half, width), jnp.bfloat16),
                pltpu.VMEM((cols, half, width), jnp.bfloat16),
            ]
            + [pltpu.VMEM((sums, cols, half, width), jnp.bfloat16)] * (levels - 2)
            + [
                pltpu.VMEM((rows, half, width), jnp.float32),
                dma((levels + 3,)),
                dma((slots,)),
                dma((slots + 2,)),
                dma((slots + 2,)),
                dma((cols,)),
                dma((cols,)),
                dma((levels - 2, sums, cols)),
                dma((levels - 2, sums, cols)),
                dma((levels - 2,)),
                dma((levels - 2,)),
                dma((rows,)),
                dma((rows,)),
                pltpu.SemaphoreType.REGULAR,
            ],
            compiler_params=pltpu.CompilerParams(
                collective_id=0, has_side_effects=True, vmem_limit_bytes=60 * 1024 * 1024
            ),
        )(tile_source, tile_target, rhs, dinv, tiles)

    placed = (
        P("groups", None, "pcol"),
        P("groups", None, "pcol"),
        P(("groups", "prow", "pcol"), None, None),
        P(("groups", "prow", "pcol")),
        P(("groups", "prow", "pcol")),
    )
    return jax.shard_map(
        body, mesh=mesh, in_specs=placed, out_specs=P("groups", None, "pcol"), check_vma=False
    )
```

```python
import jax
import jax.numpy as jnp
from jax import lax
from jax.experimental import pallas as pl
from jax.experimental.pallas import tpu as pltpu
from jax.sharding import PartitionSpec as P

MESH = pl.DeviceIdType.MESH
PAIR = 2


def apply_right(left, matrix):
    return lax.dot_general(
        left, matrix, (((1,), (1,)), ((), ())), preferred_element_type=jnp.float32
    )


def apply_plain(left, matrix):
    return jnp.dot(left, matrix, preferred_element_type=jnp.float32)


def kernel(
    cols, rows, source_hbm, target_hbm, rhs_hbm, dinv_hbm, tiles_hbm, out_hbm,
    out_ref, store_sem, source, target, rhs, dinv, raw, tiles, picked, first, halves, x0, ys, final,
    load_sem, tile_sem, send_tile, recv_tile, send_x0, recv_x0, send_y, recv_y,
    send_half, recv_half, send_final, recv_final, vouch,
):
    levels, samples = rhs.shape[0], rhs.shape[1]
    slots = raw.shape[0]
    half = samples // PAIR
    sums = rows // PAIR
    p, c = lax.axis_index("prow"), lax.axis_index("pcol")
    k, xg = lax.rem(p, PAIR), p // PAIR
    mate = p + 1 - 2 * k
    mine = pl.ds(pl.multiple_of(k * half, half), half)

    def remote(src, dst, send, recv, prow, pcol):
        return pltpu.make_async_remote_copy(
            src_ref=src, dst_ref=dst, send_sem=send, recv_sem=recv,
            device_id={"prow": prow, "pcol": pcol}, device_id_type=MESH,
        )

    side = lax.div(c, (cols + 1) // 2)
    others = []
    for t in range(cols - 1):
        down, up = cols - 1 - t, t
        down = down - lax.div(c - down + cols, cols)
        up = up + lax.div(up - c + cols, cols)
        others.append((t + 1, down + side * (up - down)))
    peers = []
    for t, pcol in others + [(0, c)]:
        for dx in range(sums - 1, -(t > 0), -1):
            peers.append((lax.rem(xg + dx, sums) * PAIR + k, pcol, dx, t))
    column = [lax.rem(p + d, rows) for d in range(1, rows)]

    load_rhs = pltpu.make_async_copy(rhs_hbm, rhs, load_sem.at[0])
    load_dinv = [
        pltpu.make_async_copy(dinv_hbm.at[level], dinv.at[level], load_sem.at[1 + level])
        for level in range(levels)
    ]
    load_source = pltpu.make_async_copy(source_hbm, source.at[0], load_sem.at[1 + levels])
    load_target = pltpu.make_async_copy(target_hbm, target.at[0], load_sem.at[2 + levels])
    load_tile = [
        pltpu.make_async_copy(tiles_hbm.at[g], raw.at[g], tile_sem.at[g])
        for g in range(slots)
    ]
    load_rhs.start()
    load_dinv[0].start()

    barrier = pltpu.get_barrier_semaphore()
    greeted = [(prow, pcol) for prow, pcol, dx, dc in peers if dx == 0]
    greeted += [(prow, c) for prow in column]
    for prow, pcol in greeted:
        pl.semaphore_signal(
            barrier, inc=1, device_id={"prow": prow, "pcol": pcol}, device_id_type=MESH
        )
    load_source.start()
    load_target.start()
    for load in load_tile + load_dinv[1:]:
        load.start()

    picked[...] = jnp.zeros_like(picked)
    load_rhs.wait()
    load_dinv[0].wait()
    block = apply_right(rhs[0], dinv[0]).astype(jnp.bfloat16)
    out_ref[0] = block
    first[...] = block
    x0[c] = first[mine]
    for g in range(slots):
        load_tile[g].wait()
        tiles[0, g] = raw[g].T
    pl.semaphore_wait(barrier, len(greeted))

    pending = []
    arrivals = []
    for prow, pcol, dx, dc in peers:
        if dx == 0:
            copy = remote(x0.at[c], x0.at[c], send_x0.at[dc], recv_x0.at[c], p, pcol)
            copy.start()
            pending.append(copy)
            arrivals.append(
                remote(x0.at[pcol], x0.at[pcol], send_x0.at[dc], recv_x0.at[pcol], p, pcol)
            )
    swap = [
        remote(source_hbm, source.at[1], send_tile.at[slots], recv_tile.at[slots], mate, c),
        remote(target_hbm, target.at[1], send_tile.at[slots + 1], recv_tile.at[slots + 1], mate, c),
    ] + [
        remote(tiles.at[0, g], tiles.at[1, g], send_tile.at[g], recv_tile.at[g], mate, c)
        for g in range(slots)
    ]
    for copy in swap:
        copy.start()
    for prow, pcol, dx, dc in peers:
        if dx and dc == 0:
            pl.semaphore_signal(
                vouch, inc=1, device_id={"prow": prow, "pcol": pcol}, device_id_type=MESH
            )
    pending += swap

    for level in range(1, levels):
        load_dinv[level].wait()
        dinv[level] = dinv[level].T
    load_source.wait()
    load_target.wait()
    swap[0].wait_recv()
    swap[1].wait_recv()
    slot = [(j, g) for j in range(PAIR) for g in range(slots)]
    src_level = {s: source[s[0], s[1]] // cols for s in slot}
    src_col = {s: lax.rem(source[s[0], s[1]], cols) for s in slot}
    to_level = {s: target[s[0], s[1]] for s in slot}

    half_copies = []
    for level in range(1, levels):
        for copy in arrivals:
            copy.wait_recv()
        partial_value = None
        for s in slot:
            if level == 1:
                if s[0] == 1:
                    swap[2 + s[1]].wait_recv()
                seen = x0[src_col[s]]
            else:
                seen = ys[level - 2][0, src_col[s]].astype(jnp.float32)
                for q in range(1, sums):
                    seen = seen + ys[level - 2][q, src_col[s]].astype(jnp.float32)
                seen = seen.astype(jnp.bfloat16)
            now = jnp.where(src_level[s] == level - 1, seen, picked[s])
            picked[s] = now
            left = jnp.where(to_level[s] == level, now, jnp.zeros_like(now))
            term = apply_plain(left, tiles[s])
            partial_value = term if partial_value is None else partial_value + term
        if level + 1 < levels:
            begin = jnp.where(xg == 0, rhs[level, mine].astype(jnp.float32), 0.0)
            short = begin - partial_value
            high = short.astype(jnp.bfloat16)
            low = (short - high.astype(jnp.float32)).astype(jnp.bfloat16)
            both = apply_plain(jnp.concatenate([high, low], axis=0), dinv[level])
            if level == 1:
                pl.semaphore_wait(vouch, sums - 1)
            y = ys[level - 1]
            y[xg, c] = (both[:half] + both[half:]).astype(jnp.bfloat16)
            arrivals = []
            for prow, pcol, dx, dc in peers:
                copy = remote(
                    y.at[xg, c], y.at[xg, c],
                    send_y.at[level - 1, dx, dc], recv_y.at[level - 1, xg, c], prow, pcol,
                )
                copy.start()
                pending.append(copy)
                q = lax.rem(xg + dx, sums)
                arrivals.append(
                    remote(
                        y.at[q, pcol], y.at[q, pcol],
                        send_y.at[level - 1, dx, dc], recv_y.at[level - 1, q, pcol], prow, pcol,
                    )
                )
        else:
            final[p] = partial_value
            arrivals = []
            for d in range(1, rows):
                copy = remote(
                    final.at[p], final.at[p], send_final.at[d], recv_final.at[d], column[d - 1], c
                )
                copy.start()
                arrivals.append(copy)
            pending += arrivals
        if level >= 2:
            y = ys[level - 2]
            total = y[0, c].astype(jnp.float32)
            for q in range(1, sums):
                total = total + y[q, c].astype(jnp.float32)
            halves[level - 2, k] = total.astype(jnp.bfloat16)
            copy = remote(
                halves.at[level - 2, k], halves.at[level - 2, k],
                send_half.at[level - 2], recv_half.at[level - 2], mate, c,
            )
            copy.start()
            half_copies.append(copy)
    for level, copy in enumerate(half_copies):
        copy.wait_recv()
        for j in range(PAIR):
            out_ref[1 + level, j * half : (j + 1) * half] = halves[level, j]
    early = pltpu.make_async_copy(
        out_ref.at[: levels - 1], out_hbm.at[: levels - 1], store_sem.at[0]
    )
    early.start()
    pending += half_copies
    for copy in arrivals:
        copy.wait_recv()
    shorts = []
    for j in range(PAIR):
        total = final[j]
        for q in range(1, sums):
            total = total + final[q * PAIR + j]
        begin = rhs[levels - 1, j * half : (j + 1) * half].astype(jnp.float32)
        shorts.append((begin - total).astype(jnp.bfloat16))
    short = jnp.concatenate(shorts, axis=0)
    out_ref[levels - 1] = apply_plain(short, dinv[levels - 1]).astype(jnp.bfloat16)
    last = pltpu.make_async_copy(out_ref.at[levels - 1], out_hbm.at[levels - 1], store_sem.at[1])
    last.start()
    for copy in pending:
        copy.wait_send()
    early.wait()
    last.wait()


def solution(mesh):
    rows, cols = mesh.shape["prow"], mesh.shape["pcol"]

    def body(rhs, dinv, tiles, tile_source, tile_target):
        levels, samples, width = rhs.shape
        slots = tiles.shape[0]
        half, sums = samples // PAIR, rows // PAIR

        def call(*refs):
            ins, scratch, rest = refs[:6], refs[6:18], refs[18:]
            ys, rest = rest[: levels - 2], rest[levels - 2 :]
            kernel(cols, rows, *ins, *scratch, ys, *rest)

        dma = pltpu.SemaphoreType.DMA
        return pl.pallas_call(
            call,
            out_shape=jax.ShapeDtypeStruct(rhs.shape, jnp.bfloat16),
            in_specs=[pl.BlockSpec(memory_space=pl.ANY)] * 5,
            out_specs=pl.BlockSpec(memory_space=pl.ANY),
            scratch_shapes=[
                pltpu.VMEM(rhs.shape, jnp.bfloat16),
                dma((2,)),
                pltpu.SMEM((PAIR, slots), jnp.int32),
                pltpu.SMEM((PAIR, slots), jnp.int32),
                pltpu.VMEM(rhs.shape, jnp.bfloat16),
                pltpu.VMEM(dinv.shape, jnp.bfloat16),
                pltpu.VMEM(tiles.shape, jnp.bfloat16),
                pltpu.VMEM((PAIR,) + tiles.shape, jnp.bfloat16),
                pltpu.VMEM((PAIR, slots, half, width), jnp.bfloat16),
                pltpu.VMEM((samples, width), jnp.bfloat16),
                pltpu.VMEM((levels - 2, PAIR, half, width), jnp.bfloat16),
                pltpu.VMEM((cols, half, width), jnp.bfloat16),
            ]
            + [pltpu.VMEM((sums, cols, half, width), jnp.bfloat16)] * (levels - 2)
            + [
                pltpu.VMEM((rows, half, width), jnp.float32),
                dma((levels + 3,)),
                dma((slots,)),
                dma((slots + 2,)),
                dma((slots + 2,)),
                dma((cols,)),
                dma((cols,)),
                dma((levels - 2, sums, cols)),
                dma((levels - 2, sums, cols)),
                dma((levels - 2,)),
                dma((levels - 2,)),
                dma((rows,)),
                dma((rows,)),
                pltpu.SemaphoreType.REGULAR,
            ],
            compiler_params=pltpu.CompilerParams(
                collective_id=0, has_side_effects=True, vmem_limit_bytes=60 * 1024 * 1024
            ),
        )(tile_source, tile_target, rhs, dinv, tiles)

    placed = (
        P("groups", None, "pcol"),
        P("groups", None, "pcol"),
        P(("groups", "prow", "pcol"), None, None),
        P(("groups", "prow", "pcol")),
        P(("groups", "prow", "pcol")),
    )
    return jax.shard_map(
        body, mesh=mesh, in_specs=placed, out_specs=P("groups", None, "pcol"), check_vma=False
    )
```
